32 devices in a mesh: groups: 2 (over x), ctx: 8 (over z, y), width: 2 (over core).
Axes of the slice: x: 2, y: 2, z: 4, core: 2. Of those that a mesh axis runs over, the one named last changes fastest.
Arguments:
- gating_vectors: bfloat16 [2048, 4096], P(('groups', 'ctx'), 'width'), parts along dimension 0, may hold values from -3 to 3
- lookup_vectors: bfloat16 [2048, 4096], P(('groups', 'ctx'), 'width'), parts along dimension 0, may hold values from -3 to 3
- payload_vectors: bfloat16 [2048, 4096], P(('groups', 'ctx'), 'width'), parts along dimension 0, may hold values from -6 to 6
- forgetting_exponent: bfloat16 [2048, 4096], P(('groups', 'ctx'), 'width'), parts along dimension 0, may hold values from 0 to 0.5
- inline_adapt_factor: bfloat16 [2048, 4096], P(('groups', 'ctx'), 'width'), parts along dimension 0, may hold values from 0 to 0.9
- group_layer_scaling: float32 [4096], P('width'), may hold values from 0.5 to 1.5
- group_layer_offset: float32 [4096], P('width'), may hold values from -3 to 3
- present_reward_factor: float32 [4096], P('width'), may hold values from -1 to 1
- shared_dictionary_matrix: bfloat16 [16384, 4096], P('ctx', 'width'), may hold values from -0.09375 to 0.09375
- sparse_code_offset: float32 [16384], P('ctx'), may hold values from -3 to 3
- reconstruct_offset: float32 [4096], P('width'), may hold values from -2 to 2
- panel_holder_choice: int32 [256, 2], P(('groups', 'ctx')), parts along dimension 0, may hold values from 0 to 7, all different within a row; in each aligned block of 16 rows (0 to 15, 16 to 31, ...) at most 8 rows name the same one
- holder_group_enabled: int32 [256, 2, 16], P(('groups', 'ctx')), parts along dimension 0, may hold values 0 or 1
- fixed_feature_slot: int32 [128], P('ctx'), may hold values from 0 to 127
- fixed_feature_amount: float32 [128], P('ctx'), may hold values from 2 to 8
Outputs:
- standardized_mixer_result: bfloat16 [2048, 4096], P(('groups', 'ctx'), 'width'), parts along dimension 0
- steered: bfloat16 [2048, 4096], P(('groups', 'ctx'), 'width'), parts along dimension 0
The draws below stay inside these ranges and needn't reach their ends.
There are 2 independent parts, one for each index of `groups`. The reference program is written for one: setup_inputs(seed, part) draws one part's arguments, and reference() takes and returns one part's arrays. A program takes and returns all parts, laid end to end along the dimension named above; an argument that names none is the same for every part. Nothing has to cross between parts.
Inputs may be any that keep to these rules, and one draw needn't show every extreme that they name: `panel_holder_choice`: each tile names 2 different owners; the tiles of one device name one owner at most 8 times, and in every draw some device's tiles name some owner exactly 8 times.
All inputs are finite; a program needn't handle non-finite values. No bound on the sum of `holder_group_enabled` on one device may be relied on, other than what follows from the above.
Results may differ from the reference program's by a relative error of at most 0.015.
Values may be sent and summed in bfloat16 or wider, within the bound.
A program may use at most 128 MiB of HBM per device.

```python
import math
import jax
import jax.numpy as jnp
import numpy as np
from jax import lax

EMBED_DIM = 4096
ATTN_GROUP_COUNT = 64
ATTN_GROUP_DIM = 64
TOK_DEV = 128
TILE = 8
OWN = 2
BLK = 128
BLK_OWN = 16
SEQUENCE_LENGTH = 1024
TILES = 128
NBLK = 128
LATENTS = 16384
CAP = 8
N_CTX = 8


def head_kinds(key):
    picked = jax.random.uniform(jax.random.fold_in(key, 11), (ATTN_GROUP_COUNT,))
    share = 0.5
    return picked < share


def draw_forgetting_exponent(key, part):
    slower_rate = head_kinds(key)
    random_splits = jax.random.split(jax.random.fold_in(key, 23), 6)
    blocks = SEQUENCE_LENGTH // TOK_DEV
    slow_rate = jnp.exp(jax.random.uniform(random_splits[0], (ATTN_GROUP_COUNT,), jnp.float32, math.log(0.03), math.log(0.12))) / SEQUENCE_LENGTH
    fast_rate = jnp.exp(jax.random.uniform(random_splits[1], (ATTN_GROUP_COUNT,), jnp.float32, math.log(1.0 / 50.0), math.log(1.0 / 30.0)))
    base = jnp.where(slower_rate, slow_rate, fast_rate)
    device_factor = jnp.exp(jax.random.uniform(random_splits[2], (blocks, ATTN_GROUP_COUNT), jnp.float32, -math.log(2.0), math.log(2.0)))
    device_factor = jnp.repeat(device_factor, TOK_DEV, axis=0)
    element_factor = jnp.exp(jax.random.uniform(random_splits[3], (SEQUENCE_LENGTH, ATTN_GROUP_COUNT, ATTN_GROUP_DIM), jnp.float32, -math.log(2.0), math.log(2.0)))
    learning_speed = base[None, :, None] * device_factor[:, :, None] * element_factor
    spike_position = jax.random.randint(random_splits[4], (2,), 0, SEQUENCE_LENGTH)
    spike_value = jax.random.uniform(random_splits[5], (ATTN_GROUP_COUNT,), jnp.float32, 0.22, 0.5)
    positions = jnp.arange(SEQUENCE_LENGTH)
    spiked_entries = jnp.any(positions[:, None] == spike_position[None, :], axis=1)
    learning_speed = jnp.where(spiked_entries[:, None, None] & slower_rate[None, :, None], spike_value[None, :, None] + 0.0 * learning_speed, learning_speed)
    return learning_speed.reshape(SEQUENCE_LENGTH, ATTN_GROUP_COUNT * ATTN_GROUP_DIM).astype(jnp.bfloat16)


def draw_inline_adapt_factor(key, part):
    slower_rate = head_kinds(key)
    moderate_heads = jax.random.uniform(jax.random.fold_in(key, 13), (ATTN_GROUP_COUNT,)) < 0.5
    random_splits = jax.random.split(jax.random.fold_in(key, 37), 3)
    small_rate = jnp.exp(jax.random.uniform(random_splits[0], (SEQUENCE_LENGTH, ATTN_GROUP_COUNT, ATTN_GROUP_DIM), jnp.float32, math.log(0.002), math.log(0.008)))
    large_rate = jax.random.uniform(random_splits[1], (SEQUENCE_LENGTH, ATTN_GROUP_COUNT, ATTN_GROUP_DIM), jnp.float32, 0.2, 0.9)
    middle_rate = jax.random.uniform(random_splits[2], (SEQUENCE_LENGTH, ATTN_GROUP_COUNT, ATTN_GROUP_DIM), jnp.float32, 0.05, 0.3)
    slow_values = jnp.where(moderate_heads[None, :, None], middle_rate, small_rate)
    learning_speed = jnp.where(slower_rate[None, :, None], slow_values, large_rate)
    return learning_speed.reshape(SEQUENCE_LENGTH, ATTN_GROUP_COUNT * ATTN_GROUP_DIM).astype(jnp.bfloat16)


def place_ends(values, key, low, high):
    place = [jax.random.randint(jax.random.fold_in(key, axis), (), 0, length) for axis, length in enumerate(values.shape)]
    main_axis = values.shape.index(max(values.shape))
    next_to = place[:main_axis] + [(place[main_axis] + 1) % values.shape[main_axis]] + place[main_axis + 1:]
    return values.at[tuple(place)].set(low).at[tuple(next_to)].set(high)


def block_scale(own_key, shape, cuts, smallest, high):
    factor_of = 1.0
    for dim, shards_of in cuts:
        steps = jax.random.uniform(jax.random.fold_in(jax.random.fold_in(own_key, 6), dim), (shards_of,), jnp.float32, smallest / len(cuts), high / len(cuts))
        factor_of = factor_of * jnp.repeat(jnp.exp(steps), shape[dim] // shards_of).reshape((-1,) + (1,) * (len(shape) - 1 - dim))
    return factor_of


def routed_block(own_key, own, number, rows, number_of, top, limit, skew):
    ranking = jax.random.permutation(own_key, number_of)
    packed, usual = shares(number_of, rows * top, limit, skew, True), shares(number_of, rows * top, limit, skew, False)
    places = jnp.arange(number_of)

    def named(sizes, rotation):
        used = int((sizes > 0).sum())
        fixed = max(1, used // 4)
        passed = fixed + (places - fixed + rotation * (used - fixed)) % max(1, number_of - fixed)
        return jnp.zeros((number_of,), jnp.int32).at[ranking[jnp.where(places < fixed, places, passed)]].set(jnp.asarray(sizes, jnp.int32))

    sizes = jnp.where(number % 4 == 0, named(packed, number // 4), named(usual, number - number // 4 - 1))
    mixed = jax.random.permutation(jax.random.fold_in(own, 3), number_of)
    donor, receiver = mixed[0:number_of // 2 * 2:2], mixed[1:number_of // 2 * 2:2]
    slack = jnp.minimum(sizes[donor] - 1, limit - sizes[receiver]) // 2
    slack = jnp.where((donor == ranking[0]) | (receiver == ranking[0]) | (sizes[receiver] == 0), 0, jnp.maximum(slack, 0))
    passed = jax.random.randint(jax.random.fold_in(own, 4), (number_of // 2,), 0, 1 << 20) % (slack + 1)
    sizes = sizes.at[donor].add(-passed).at[receiver].add(passed)
    labels = jnp.searchsorted(jnp.cumsum(sizes), jnp.arange(rows * top), side="right").astype(jnp.int32)
    table = labels.reshape(top, rows).T
    table = table[jax.random.permutation(jax.random.fold_in(own, 1), rows)]
    rotation = jax.random.randint(jax.random.fold_in(own, 2), (rows, 1), 0, top)
    return jnp.take_along_axis(table, (jnp.arange(top)[None, :] + rotation) % top, axis=1)


def shares(number_of, total, bound, slope, full):
    portions = [(1 << 20) // math.isqrt(rank ** slope) + 1 for rank in range(1, number_of + 1)]
    largest = bound if full else min(bound, max(-(-total // number_of), total * portions[0] // sum(portions)))
    least = 1 if total - largest >= number_of - 1 else 0
    given, spare = [largest] + [least] * (number_of - 1), total - largest - least * (number_of - 1)
    while spare > 0:
        candidates = [i for i in range(1, number_of) if given[i] < largest] or [i for i in range(1, number_of) if given[i] < bound]
        mass, left = sum([portions[i] for i in candidates]), spare
        for i in candidates:
            more = min(bound - given[i], max(1, left * portions[i] // mass), spare)
            given[i] = given[i] + more
            spare = spare - more
    return np.array(given)


def noise(rng, shape, scale, bound, cuts=(), held_as=jnp.bfloat16):
    gain = block_scale(rng, shape, cuts, -0.22, 0.18) if cuts else 1.0
    array = jax.random.normal(rng, shape, jnp.float32) * scale * gain
    return jnp.minimum(jnp.maximum(array, -bound), bound).astype(held_as)


def setup_inputs(seed: int = 0, part: int = 0) -> dict:
    streams_of = jax.random.split(jax.random.key(seed), 16)
    own_keys = jax.random.split(jax.random.fold_in(streams_of[15], part), 16)
    gating_vectors = noise(own_keys[0], (SEQUENCE_LENGTH, EMBED_DIM), 0.5, 3.0, ((0, 8), (1, 2)))
    lookup_vectors = noise(own_keys[1], (SEQUENCE_LENGTH, EMBED_DIM), 0.5, 3.0, ((0, 8), (1, 2)))
    payload_vectors = noise(own_keys[2], (SEQUENCE_LENGTH, EMBED_DIM), 1.0, 6.0, ((0, 8), (1, 2)))
    forgetting_exponent = draw_forgetting_exponent(jax.random.fold_in(jax.random.fold_in(streams_of[15], part), 71), part)
    inline_adapt_factor = draw_inline_adapt_factor(jax.random.fold_in(jax.random.fold_in(streams_of[15], part), 71), part)
    group_layer_scaling = jnp.clip(0.5 + 1.0 * jax.random.uniform(streams_of[5], (EMBED_DIM,), jnp.float32) ** block_scale(streams_of[5], (EMBED_DIM,), ((0, 2),), -0.2, 0.2), 0.5, 1.5)
    group_layer_offset = noise(streams_of[6], (EMBED_DIM,), 0.5, 3.0, ((0, 2),), jnp.float32)
    present_reward_factor = jnp.clip(jax.random.uniform(streams_of[7], (EMBED_DIM,), jnp.float32, -1.0, 1.0) * block_scale(streams_of[7], (EMBED_DIM,), ((0, 2),), -0.4, 0.0), -1.0, 1.0)
    shared_dictionary_matrix = noise(streams_of[8], (LATENTS, EMBED_DIM), EMBED_DIM ** -0.5, 0.09375, ((0, 8), (1, 2)))
    sparse_code_offset = noise(streams_of[9], (LATENTS,), 0.5, 3.0, ((0, 8),), jnp.float32)
    reconstruct_offset = noise(streams_of[10], (EMBED_DIM,), 0.3, 2.0, ((0, 2),), jnp.float32)
    panel_holder_choice_keys = jax.random.split(jax.random.fold_in(own_keys[11], 1), TILES // (TOK_DEV // TILE))
    panel_holder_choice_turns = jax.random.permutation(jax.random.fold_in(own_keys[11], 3), TILES // (TOK_DEV // TILE))
    panel_holder_choice = jax.vmap(lambda own, number: routed_block(jax.random.fold_in(own_keys[11], 2), own, number, TOK_DEV // TILE, N_CTX, OWN, CAP, 1))(panel_holder_choice_keys, panel_holder_choice_turns).reshape((TILES, OWN))
    holder_group_enabled = place_ends((jax.random.randint(own_keys[12], (TILES, OWN, BLK_OWN), 0, 2) < 1).astype(jnp.int32), jax.random.fold_in(own_keys[12], 1), 0, 1)
    fixed_feature_slot = place_ends(jax.random.randint(streams_of[13], (NBLK,), 0, BLK), jax.random.fold_in(streams_of[13], 1), 0, BLK - 1).astype(jnp.int32)
    fixed_feature_amount = jnp.clip(2.0 + 6.0 * jax.random.uniform(streams_of[14], (NBLK,), jnp.float32) ** block_scale(streams_of[14], (NBLK,), ((0, 8),), -0.2, 0.2), 2.0, 8.0)
    return dict(gating_vectors=gating_vectors, lookup_vectors=lookup_vectors, payload_vectors=payload_vectors, forgetting_exponent=forgetting_exponent, inline_adapt_factor=inline_adapt_factor, group_layer_scaling=group_layer_scaling, group_layer_offset=group_layer_offset, present_reward_factor=present_reward_factor, shared_dictionary_matrix=shared_dictionary_matrix, sparse_code_offset=sparse_code_offset, reconstruct_offset=reconstruct_offset, panel_holder_choice=panel_holder_choice, holder_group_enabled=holder_group_enabled, fixed_feature_slot=fixed_feature_slot, fixed_feature_amount=fixed_feature_amount)


def reference(gating_vectors, lookup_vectors, payload_vectors, forgetting_exponent, inline_adapt_factor, group_layer_scaling, group_layer_offset, present_reward_factor, shared_dictionary_matrix, sparse_code_offset, reconstruct_offset, panel_holder_choice, holder_group_enabled, fixed_feature_slot, fixed_feature_amount):
    highest = lax.Precision.HIGHEST
    gating_vectors_all = gating_vectors.astype(jnp.float32).reshape(SEQUENCE_LENGTH, ATTN_GROUP_COUNT, ATTN_GROUP_DIM)
    lookup_vectors_all = lookup_vectors.astype(jnp.float32).reshape(SEQUENCE_LENGTH, ATTN_GROUP_COUNT, ATTN_GROUP_DIM)
    payload_vectors_all = payload_vectors.astype(jnp.float32).reshape(SEQUENCE_LENGTH, ATTN_GROUP_COUNT, ATTN_GROUP_DIM)
    decay_all = jnp.exp(-forgetting_exponent.astype(jnp.float32)).reshape(SEQUENCE_LENGTH, ATTN_GROUP_COUNT, ATTN_GROUP_DIM)
    learn_all = inline_adapt_factor.astype(jnp.float32).reshape(SEQUENCE_LENGTH, ATTN_GROUP_COUNT, ATTN_GROUP_DIM)
    removal = lookup_vectors_all * lax.rsqrt(lax.optimization_barrier(jnp.sum(lookup_vectors_all * lookup_vectors_all, -1, keepdims=True)) + ATTN_GROUP_DIM * 1e-05)

    def advance(carried, pieces):
        rec_t, key_t, val_t, decay_t, removal_t, learn_t = pieces
        erased = jnp.einsum('hvk,hk->hv', carried, removal_t, precision=highest)
        carried = carried * decay_t[:, None, :] - erased[:, :, None] * (removal_t * learn_t)[:, None, :] + val_t[:, :, None] * key_t[:, None, :]
        output = jnp.einsum('hvk,hk->hv', carried, rec_t, precision=highest)
        return (carried, output)
    _, wkv = lax.scan(advance, jnp.zeros((ATTN_GROUP_COUNT, ATTN_GROUP_DIM, ATTN_GROUP_DIM), jnp.float32), (gating_vectors_all, lookup_vectors_all, payload_vectors_all, decay_all, removal, learn_all))
    center = wkv - lax.optimization_barrier(jnp.mean(wkv, -1, keepdims=True))
    spread = lax.optimization_barrier(jnp.mean(center * center, -1, keepdims=True))
    standardized_lines = (center * lax.rsqrt(spread + 1e-05)).reshape(SEQUENCE_LENGTH, EMBED_DIM) * group_layer_scaling + group_layer_offset
    present_reward = (lax.optimization_barrier(jnp.sum(gating_vectors_all * lookup_vectors_all * present_reward_factor.reshape(ATTN_GROUP_COUNT, ATTN_GROUP_DIM), -1, keepdims=True)) * payload_vectors_all).reshape(SEQUENCE_LENGTH, EMBED_DIM)
    standardized_mixer_result = (standardized_lines + present_reward).astype(jnp.bfloat16)
    enc_in = (standardized_mixer_result.astype(jnp.float32) - reconstruct_offset).astype(jnp.bfloat16)
    lat_own = BLK * BLK_OWN
    tile_in = enc_in.reshape(TILES, TILE, EMBED_DIM)
    within = lax.broadcasted_iota(jnp.int32, (BLK_OWN, BLK), 1)

    def one_tile(pieces):
        tile_rows, owners, masks = pieces
        total = jnp.zeros((TILE, EMBED_DIM), jnp.float32)
        for slot_idx in range(OWN):
            first = (owners[slot_idx] * lat_own).astype(jnp.int32)
            first_blk = (owners[slot_idx] * BLK_OWN).astype(jnp.int32)
            weights = lax.dynamic_slice_in_dim(shared_dictionary_matrix, first, lat_own, 0)
            biases = lax.dynamic_slice_in_dim(sparse_code_offset, first, lat_own, 0)
            chosen = lax.dynamic_slice_in_dim(fixed_feature_slot, first_blk, BLK_OWN, 0)
            forced = lax.dynamic_slice_in_dim(fixed_feature_amount, first_blk, BLK_OWN, 0)
            preact = lax.dot_general(tile_rows, weights, (((1,), (1,)), ((), ())), preferred_element_type=jnp.float32) + biases
            code = jnp.maximum(preact, 0.0).reshape(TILE, BLK_OWN, BLK)
            hit = within == chosen[:, None]
            code = jnp.where(hit[None], forced[None, :, None], code)
            code = (code * masks[slot_idx].astype(jnp.float32)[None, :, None]).reshape(TILE, lat_own).astype(jnp.bfloat16)
            part = jnp.dot(code, weights, preferred_element_type=jnp.float32).astype(jnp.bfloat16)
            total = total + part.astype(jnp.float32)
        return (total + reconstruct_offset).astype(jnp.bfloat16)
    steered = lax.map(one_tile, (tile_in, panel_holder_choice, holder_group_enabled)).reshape(SEQUENCE_LENGTH, EMBED_DIM)
    return (standardized_mixer_result, steered)
```

```python
import functools

import jax
import jax.numpy as jnp
from jax import lax
from jax.experimental import pallas as pl
from jax.experimental.pallas import tpu as pltpu
from jax.sharding import PartitionSpec as P

ATTN_GROUP_DIM = 64
TILE = 8
BLK = 128
LANES = 128
PAIRS = 2

HIGHEST = lax.Precision.HIGHEST
BF16 = jnp.bfloat16
F32 = jnp.float32
ROWS_COLS = (((1,), (0,)), ((), ()))
COLS_COLS = (((1,), (1,)), ((), ()))
ROWS_ROWS = (((0,), (0,)), ((), ()))


def once(a, b, dims=ROWS_COLS):
    return lax.dot_general(a.astype(BF16), b.astype(BF16), dims, preferred_element_type=F32)


def split(a):
    high = a.astype(BF16)
    return high, (a - high.astype(F32)).astype(BF16)


def thrice(a, b, dims=ROWS_COLS):
    a_high, a_low = split(a)
    b_high, b_low = split(b)
    dot = functools.partial(lax.dot_general, dimension_numbers=dims, preferred_element_type=F32)
    return dot(a_high, b_high) + (dot(a_high, b_low) + dot(a_low, b_high))


def iota(shape, dim):
    return lax.broadcasted_iota(jnp.int32, shape, dim)


def head_sum(array, first):
    low = jnp.sum(jnp.where(first, array, 0.0), -1, keepdims=True)
    high = jnp.sum(jnp.where(first, 0.0, array), -1, keepdims=True)
    return jnp.where(first, low, high)


def mixer_kernel(
    devices,
    rec_ref,
    key_ref,
    val_ref,
    rate_ref,
    learn_ref,
    scale_ref,
    shift_ref,
    reward_ref,
    center_ref,
    mixed_ref,
    enc_ref,
    local_s,
    probe_s,
    trans_s,
    own_s,
    arrive_s,
    leave_s,
    send_sem,
    recv_sem,
):
    me = lax.axis_index("ctx")
    tokens, width = rec_ref.shape
    chunk_lanes = PAIRS * LANES
    chunks = width // chunk_lanes

    barrier = pltpu.get_barrier_semaphore()
    for other in (lax.rem(me + 1, devices), lax.rem(me + devices - 1, devices)):
        pl.semaphore_signal(
            barrier, inc=1, device_id={"ctx": other}, device_id_type=pl.DeviceIdType.MESH
        )
    pl.semaphore_wait(barrier, 2)

    def lanes_of(chunk, pair):
        return pl.ds(pl.multiple_of(chunk * chunk_lanes + pair * LANES, LANES), LANES)

    def onward(chunk):
        return pltpu.make_async_remote_copy(
            src_ref=leave_s.at[chunk],
            dst_ref=arrive_s.at[chunk],
            send_sem=send_sem.at[chunk],
            recv_sem=recv_sem.at[chunk],
            device_id={"ctx": me + 1},
            device_id_type=pl.DeviceIdType.MESH,
        )

    def local(chunk):
        first = iota((tokens, LANES), 1) < ATTN_GROUP_DIM
        row = iota((tokens, tokens), 0)
        col = iota((tokens, tokens), 1)
        strict = row > col
        inclusive = row >= col
        same_head = (iota((LANES, LANES), 0) < ATTN_GROUP_DIM) == (
            iota((LANES, LANES), 1) < ATTN_GROUP_DIM
        )
        diagonal = iota((LANES, LANES), 0) == iota((LANES, LANES), 1)
        lower = inclusive.astype(F32).astype(BF16)
        identity = (row == col).astype(F32)

        todo = []
        for pair in range(PAIRS):
            at = lanes_of(chunk, pair)
            rec = rec_ref[:, at].astype(F32)
            key = key_ref[:, at].astype(F32)
            val = val_ref[:, at].astype(F32)
            rate = rate_ref[:, at].astype(F32)
            learn = learn_ref[:, at].astype(F32)
            total = lax.dot_general(
                lower, rate_ref[:, at], ROWS_COLS, preferred_element_type=F32
            )
            removal = key * lax.rsqrt(head_sum(key * key, first) + ATTN_GROUP_DIM * 1e-05)
            undo = jnp.exp(total)
            fade_to_end = jnp.exp(total - total[tokens - 1 :, :])
            left_a = -removal * jnp.exp(rate - total)
            left_r = rec * jnp.exp(-total)
            erase = removal * learn
            right = jnp.concatenate([erase * undo, key * undo], 0)
            ends = jnp.concatenate([erase * fade_to_end, key * fade_to_end], 0)
            fade = jnp.exp(-total[tokens - 1 :, :])
            sides = []
            for head in range(2):
                mine = first if head == 0 else jnp.logical_not(first)
                left = jnp.concatenate(
                    [jnp.where(mine, left_a, 0.0), jnp.where(mine, left_r, 0.0)], 0
                )
                gram = once(left, right, COLS_COLS)
                mix_ab = jnp.where(strict, gram[:tokens, :tokens], 0.0)
                mix_ak = jnp.where(strict, gram[:tokens, tokens:], 0.0)
                mix_rb = jnp.where(inclusive, gram[tokens:, :tokens], 0.0)
                mix_rk = jnp.where(inclusive, gram[tokens:, tokens:], 0.0)
                own_val = jnp.where(mine, val, 0.0)
                target = jnp.concatenate(
                    [once(mix_ak, own_val), jnp.where(mine, left_a, 0.0)], 1
                )
                sides.append((mix_ab, mix_rb, mix_rk, own_val, target))
            todo.append((at, left_r, val, ends, fade, sides))

        inverse = []
        for work in todo:
            for side in work[5]:
                pick = (row // 2 == col // 2)
                inverse.append(identity + jnp.where(pick, side[0], 0.0))
        size = 2
        while size < tokens:
            pick = (row // (2 * size) == col // (2 * size)) & (row // size != col // size)
            step = []
            index = 0
            for work in todo:
                for side in work[5]:
                    step.append(MM(inverse[index], jnp.where(pick, side[0], 0.0)))
                    index += 1
            inverse = [now + MM(part, now) for now, part in zip(inverse, step)]
            size *= 2

        for pair, (at, left_r, val, ends, fade, sides) in enumerate(todo):
            reads = [MM(inverse[2 * pair + head], sides[head][4]) for head in range(2)]
            both = reads[0] + reads[1]
            outs = once(
                jnp.concatenate([sides[0][1], sides[1][1]], 1), jnp.concatenate(reads, 0)
            )
            straight = once(
                jnp.concatenate([sides[0][2], sides[1][2]], 1),
                jnp.concatenate([sides[0][3], sides[1][3]], 0),
            )
            local_s[:, at] = outs[:, :LANES] + straight
            probe_s[:, at] = outs[:, LANES:] + left_r
            carry = once(both[:, LANES:], ends[:tokens], ROWS_ROWS)
            spot = chunk * PAIRS + pair
            trans_s[spot] = jnp.where(same_head, carry, 0.0) + jnp.where(diagonal, fade, 0.0)
            made = once(jnp.concatenate([both[:, :LANES], val], 0), ends, ROWS_ROWS)
            made = jnp.where(same_head, made, 0.0)
            own_s[spot] = made[:ATTN_GROUP_DIM] + made[ATTN_GROUP_DIM:]

    def finish(chunk):
        first = iota((tokens, LANES), 1) < ATTN_GROUP_DIM
        same_head = (iota((LANES, LANES), 0) < ATTN_GROUP_DIM) == (
            iota((LANES, LANES), 1) < ATTN_GROUP_DIM
        )
        for pair in range(PAIRS):
            at = lanes_of(chunk, pair)
            prior = arrive_s[chunk, pair]
            prior = jnp.where(same_head, jnp.concatenate([prior, prior], 0), 0.0)
            wkv = local_s[:, at] + once(probe_s[:, at], prior, COLS_COLS)
            center = wkv - head_sum(wkv, first) * (1.0 / ATTN_GROUP_DIM)
            spread = head_sum(center * center, first) * (1.0 / ATTN_GROUP_DIM)
            lines = center * lax.rsqrt(spread + 1e-05) * scale_ref[:, at] + shift_ref[:, at]
            bonus = head_sum(
                rec_ref[:, at].astype(F32) * key_ref[:, at].astype(F32) * reward_ref[:, at], first
            ) * val_ref[:, at].astype(F32)
            mixed = (lines + bonus).astype(BF16)
            mixed_ref[:, at] = mixed
            enc_ref[:, at] = (mixed.astype(F32) - center_ref[:, at]).astype(BF16)

    def chain(chunk):
        @pl.when(me == 0)
        def _():
            arrive_s[chunk] = jnp.zeros(arrive_s.shape[1:], F32)

        @pl.when(me > 0)
        def _():
            onward(chunk).wait_recv()

        @pl.when(me < devices - 1)
        def _():
            for pair in range(PAIRS):
                spot = chunk * PAIRS + pair
                leave_s[chunk, pair] = (
                    thrice(arrive_s[chunk, pair], trans_s[spot]) + own_s[spot]
                )
            onward(chunk).start()

        finish(chunk)

    def step(index, _):
        @pl.when(index < chunks)
        def _():
            local(index)

        late = index - me

        @pl.when((late >= 0) & (late < chunks))
        def _():
            chain(late)

        return 0

    lax.fori_loop(0, chunks + devices - 1, step, 0)

    @pl.when(me < devices - 1)
    def _():
        def drain(chunk, _):
            onward(chunk).wait_send()
            return 0

        lax.fori_loop(0, chunks, drain, 0)


MM = thrice


def mixer(devices, rec, key, val, rate, learn, scale, shift, reward, center):
    tokens, width = rec.shape
    chunks = width // (PAIRS * LANES)
    pairs = width // LANES
    shape = jax.ShapeDtypeStruct((tokens, width), BF16)
    vmem = pl.BlockSpec(memory_space=pltpu.VMEM)
    return pl.pallas_call(
        functools.partial(mixer_kernel, devices),
        out_shape=(shape, shape),
        in_specs=[vmem] * 9,
        out_specs=(vmem, vmem),
        scratch_shapes=[
            pltpu.VMEM((tokens, width), F32),
            pltpu.VMEM((tokens, width), F32),
            pltpu.VMEM((pairs, LANES, LANES), F32),
            pltpu.VMEM((pairs, ATTN_GROUP_DIM, LANES), F32),
            pltpu.VMEM((chunks, PAIRS, ATTN_GROUP_DIM, LANES), F32),
            pltpu.VMEM((chunks, PAIRS, ATTN_GROUP_DIM, LANES), F32),
            pltpu.SemaphoreType.DMA((chunks,)),
            pltpu.SemaphoreType.DMA((chunks,)),
        ],
        compiler_params=pltpu.CompilerParams(
            collective_id=0, has_side_effects=True, vmem_limit_bytes=40 * 1024 * 1024
        ),
        name="mixer",
    )(rec, key, val, rate, learn, scale[None], shift[None], reward[None], center[None])


def activate(preacts, mask_vals, index_vals, value_vals):
    senders, items, block_count = mask_vals.shape
    codes = jnp.maximum(preacts, 0.0).reshape(senders, items, TILE, block_count, BLK)
    within = lax.broadcasted_iota(jnp.int32, (block_count, BLK), 1)
    hit = within == index_vals[:, None]
    codes = jnp.where(hit, value_vals[:, None], codes)
    codes = codes * mask_vals.astype(jnp.float32)[:, :, None, :, None]
    return codes.reshape(senders * items * TILE, block_count * BLK).astype(jnp.bfloat16)


def body(
    gating_vectors,
    lookup_vectors,
    payload_vectors,
    forgetting_exponent,
    inline_adapt_factor,
    group_layer_scaling,
    group_layer_offset,
    present_reward_factor,
    shared_dictionary_matrix,
    sparse_code_offset,
    reconstruct_offset,
    panel_holder_choice,
    holder_group_enabled,
    fixed_feature_slot,
    fixed_feature_amount,
):
    tok_rows = gating_vectors.shape[0]
    feat_local = gating_vectors.shape[1]
    standardized_mixer_result, enc_in = mixer(
        lax.axis_size("ctx"),
        gating_vectors,
        lookup_vectors,
        payload_vectors,
        forgetting_exponent,
        inline_adapt_factor,
        group_layer_scaling,
        group_layer_offset,
        present_reward_factor,
        reconstruct_offset,
    )
    ctx_count = lax.axis_size("ctx")
    tile_count = tok_rows // TILE
    slot_count = panel_holder_choice.shape[1]
    blocks_own = holder_group_enabled.shape[2]
    capacity = max(2, 2 * tok_rows * slot_count // (TILE * ctx_count))
    pair_count = tile_count * slot_count
    owner_flat = panel_holder_choice.reshape(pair_count)
    earlier = (owner_flat[:, None] == owner_flat[None, :]) & (
        iota((pair_count, pair_count), 1) < iota((pair_count, pair_count), 0)
    )
    ranks = jnp.sum(earlier.astype(jnp.int32), axis=1)
    slot_ids = owner_flat * capacity + ranks
    dispatch = (
        slot_ids[None, :] == lax.broadcasted_iota(jnp.int32, (ctx_count * capacity, 1), 0)
    ).astype(jnp.float32)
    tile_pick = (
        lax.broadcasted_iota(jnp.int32, (tile_count, pair_count), 1) // slot_count
        == lax.broadcasted_iota(jnp.int32, (tile_count, pair_count), 0)
    ).astype(jnp.float32)
    slot_tile = jnp.dot(dispatch, tile_pick.T)
    send_rows = jnp.dot(
        slot_tile.astype(jnp.bfloat16),
        enc_in.reshape(tile_count, TILE * feat_local),
        preferred_element_type=jnp.float32,
    )
    send_rows = send_rows.astype(jnp.bfloat16).reshape(ctx_count, capacity, TILE, feat_local)
    send_mask = jnp.dot(
        dispatch, holder_group_enabled.reshape(pair_count, blocks_own).astype(jnp.float32)
    )
    send_mask = send_mask.astype(jnp.bfloat16).reshape(ctx_count, capacity, blocks_own)
    got_rows = lax.all_to_all(send_rows, "ctx", split_axis=0, concat_axis=0, tiled=True)
    got_mask = lax.all_to_all(send_mask, "ctx", split_axis=0, concat_axis=0, tiled=True)
    senders = got_rows.shape[0]
    items = got_rows.shape[1]
    flat_rows = got_rows.reshape(senders * items * TILE, feat_local)
    partial_pre = lax.dot_general(
        flat_rows,
        shared_dictionary_matrix,
        (((1,), (1,)), ((), ())),
        preferred_element_type=jnp.float32,
    )
    total_pre = lax.psum(partial_pre.astype(jnp.bfloat16), "width").astype(jnp.float32)
    codes = activate(
        total_pre + sparse_code_offset, got_mask, fixed_feature_slot, fixed_feature_amount
    )
    decoded = jnp.dot(codes, shared_dictionary_matrix, preferred_element_type=jnp.float32).astype(
        jnp.bfloat16
    )
    returned = decoded.reshape(senders, items, TILE, feat_local)
    received = lax.all_to_all(returned, "ctx", split_axis=0, concat_axis=0, tiled=True)
    summed = jnp.dot(
        slot_tile.T.astype(jnp.bfloat16),
        received.reshape(ctx_count * capacity, TILE * feat_local),
        preferred_element_type=jnp.float32,
    )
    steered = (summed.reshape(tok_rows, feat_local) + reconstruct_offset).astype(jnp.bfloat16)
    return (standardized_mixer_result, steered)


def solution(mesh):
    placed = (
        P(("groups", "ctx"), "width"),
        P(("groups", "ctx"), "width"),
        P(("groups", "ctx"), "width"),
        P(("groups", "ctx"), "width"),
        P(("groups", "ctx"), "width"),
        P("width"),
        P("width"),
        P("width"),
        P("ctx", "width"),
        P("ctx"),
        P("width"),
        P(("groups", "ctx"), None),
        P(("groups", "ctx"), None, None),
        P("ctx"),
        P("ctx"),
    )
    return jax.shard_map(
        body,
        mesh=mesh,
        in_specs=placed,
        out_specs=(P(("groups", "ctx"), "width"), P(("groups", "ctx"), "width")),
        check_vma=False,
    )
```

```python
import functools

import jax
import jax.numpy as jnp
from jax import lax
from jax.experimental import pallas as pl
from jax.experimental.pallas import tpu as pltpu
from jax.sharding import PartitionSpec as P

ATTN_GROUP_DIM = 64
TILE = 8
BLK = 128
LANES = 128
PAIRS = 2

HIGHEST = lax.Precision.HIGHEST
BF16 = jnp.bfloat16
F32 = jnp.float32
ROWS_COLS = (((1,), (0,)), ((), ()))
COLS_COLS = (((1,), (1,)), ((), ()))
ROWS_ROWS = (((0,), (0,)), ((), ()))


def once(a, b, dims=ROWS_COLS):
    return lax.dot_general(a.astype(BF16), b.astype(BF16), dims, preferred_element_type=F32)


def split(a):
    high = a.astype(BF16)
    return high, (a - high.astype(F32)).astype(BF16)


def thrice(a, b, dims=ROWS_COLS):
    a_high, a_low = split(a)
    b_high, b_low = split(b)
    dot = functools.partial(lax.dot_general, dimension_numbers=dims, preferred_element_type=F32)
    return dot(a_high, b_high) + (dot(a_high, b_low) + dot(a_low, b_high))


def iota(shape, dim):
    return lax.broadcasted_iota(jnp.int32, shape, dim)


def head_sum(array, first):
    low = jnp.sum(jnp.where(first, array, 0.0), -1, keepdims=True)
    high = jnp.sum(jnp.where(first, 0.0, array), -1, keepdims=True)
    return jnp.where(first, low, high)


def whole_kernel(
    devices,
    rec_ref,
    key_ref,
    val_ref,
    rate_ref,
    learn_ref,
    scale_ref,
    shift_ref,
    reward_ref,
    center_ref,
    spread_ref,
    gather_ref,
    tile_mask_ref,
    bias_ref,
    hit_ref,
    forced_ref,
    table_ref,
    mixed_ref,
    steered_ref,
    local_s,
    probe_s,
    trans_s,
    own_s,
    arrive_s,
    leave_s,
    table_s,
    stage_s,
    got_s,
    mask_s,
    pre_s,
    half_s,
    peer_s,
    codes_s,
    part_s,
    back_s,
    send_sem,
    recv_sem,
    table_sem,
    out_sem,
    in_sem,
    mask_out_sem,
    mask_in_sem,
    half_out_sem,
    half_in_sem,
    part_out_sem,
    part_in_sem,
):
    me = lax.axis_index("ctx")
    peer = 1 - lax.axis_index("width")
    tokens, width = rec_ref.shape
    chunk_lanes = PAIRS * LANES
    chunks = width // chunk_lanes
    latents = bias_ref.shape[1]
    rows = spread_ref.shape[0]
    pair_rows = rows // devices
    strips = latents // STRIP

    table_copy = pltpu.make_async_copy(table_ref, table_s, table_sem)
    table_copy.start()

    barrier = pltpu.get_barrier_semaphore()

    def greet(hop, _):
        pl.semaphore_signal(
            barrier,
            inc=1,
            device_id={"ctx": lax.rem(me + hop, devices)},
            device_id_type=pl.DeviceIdType.MESH,
        )
        return 0

    lax.fori_loop(1, devices, greet, 0)
    pl.semaphore_signal(
        barrier, inc=1, device_id={"width": peer}, device_id_type=pl.DeviceIdType.MESH
    )
    pl.semaphore_wait(barrier, devices)

    def mask_copy(source, owner, sender):
        return pltpu.make_async_remote_copy(
            src_ref=tile_mask_ref.at[source],
            dst_ref=mask_s.at[sender],
            send_sem=mask_out_sem.at[owner],
            recv_sem=mask_in_sem.at[sender],
            device_id={"ctx": owner},
            device_id_type=pl.DeviceIdType.MESH,
        )

    def row_copy(chunk, owner, sender):
        return pltpu.make_async_remote_copy(
            src_ref=stage_s.at[chunk, owner],
            dst_ref=got_s.at[chunk, sender],
            send_sem=out_sem.at[chunk, owner],
            recv_sem=in_sem.at[chunk, sender],
            device_id={"ctx": owner},
            device_id_type=pl.DeviceIdType.MESH,
        )

    def part_copy(chunk, home, owner):
        return pltpu.make_async_remote_copy(
            src_ref=part_s.at[chunk, home],
            dst_ref=back_s.at[chunk, owner],
            send_sem=part_out_sem.at[chunk, home],
            recv_sem=part_in_sem.at[chunk, owner],
            device_id={"ctx": home},
            device_id_type=pl.DeviceIdType.MESH,
        )

    def half_copy(strip):
        return pltpu.make_async_remote_copy(
            src_ref=half_s.at[strip],
            dst_ref=peer_s.at[strip],
            send_sem=half_out_sem.at[strip],
            recv_sem=half_in_sem.at[strip],
            device_id={"width": peer},
            device_id_type=pl.DeviceIdType.MESH,
        )

    def others(visit):
        def hop_to(hop, _):
            visit(lax.rem(me + hop, devices))
            return 0

        lax.fori_loop(1, devices, hop_to, 0)

    others(lambda other: mask_copy(other, other, me).start())
    mask_s[me] = tile_mask_ref[me]

    def lanes_of(chunk, pair):
        return pl.ds(pl.multiple_of(chunk * chunk_lanes + pair * LANES, LANES), LANES)

    def onward(chunk):
        return pltpu.make_async_remote_copy(
            src_ref=leave_s.at[chunk],
            dst_ref=arrive_s.at[chunk],
            send_sem=send_sem.at[chunk],
            recv_sem=recv_sem.at[chunk],
            device_id={"ctx": me + 1},
            device_id_type=pl.DeviceIdType.MESH,
        )

    def local(chunk):
        first = iota((tokens, LANES), 1) < ATTN_GROUP_DIM
        row = iota((tokens, tokens), 0)
        col = iota((tokens, tokens), 1)
        strict = row > col
        inclusive = row >= col
        same_head = (iota((LANES, LANES), 0) < ATTN_GROUP_DIM) == (
            iota((LANES, LANES), 1) < ATTN_GROUP_DIM
        )
        diagonal = iota((LANES, LANES), 0) == iota((LANES, LANES), 1)
        lower = inclusive.astype(F32).astype(BF16)
        identity = (row == col).astype(F32)

        todo = []
        for pair in range(PAIRS):
            at = lanes_of(chunk, pair)
            rec = rec_ref[:, at].astype(F32)
            key = key_ref[:, at].astype(F32)
            val = val_ref[:, at].astype(F32)
            rate = rate_ref[:, at].astype(F32)
            learn = learn_ref[:, at].astype(F32)
            total = lax.dot_general(
                lower, rate_ref[:, at], ROWS_COLS, preferred_element_type=F32
            )
            removal = key * lax.rsqrt(head_sum(key * key, first) + ATTN_GROUP_DIM * 1e-05)
            undo = jnp.exp(total)
            fade_to_end = jnp.exp(total - total[tokens - 1 :, :])
            left_a = -removal * jnp.exp(rate - total)
            left_r = rec * jnp.exp(-total)
            erase = removal * learn
            right = jnp.concatenate([erase * undo, key * undo], 0)
            ends = jnp.concatenate([erase * fade_to_end, key * fade_to_end], 0)
            fade = jnp.exp(-total[tokens - 1 :, :])
            sides = []
            for head in range(2):
                mine = first if head == 0 else jnp.logical_not(first)
                left = jnp.concatenate(
                    [jnp.where(mine, left_a, 0.0), jnp.where(mine, left_r, 0.0)], 0
                )
                gram = once(left, right, COLS_COLS)
                mix_ab = jnp.where(strict, gram[:tokens, :tokens], 0.0)
                mix_ak = jnp.where(strict, gram[:tokens, tokens:], 0.0)
                mix_rb = jnp.where(inclusive, gram[tokens:, :tokens], 0.0)
                mix_rk = jnp.where(inclusive, gram[tokens:, tokens:], 0.0)
                own_val = jnp.where(mine, val, 0.0)
                target = jnp.concatenate(
                    [once(mix_ak, own_val), jnp.where(mine, left_a, 0.0)], 1
                )
                sides.append((mix_ab, mix_rb, mix_rk, own_val, target))
            todo.append((at, left_r, val, ends, fade, sides))

        inverse = []
        for work in todo:
            for side in work[5]:
                pick = (row // 2 == col // 2)
                inverse.append(identity + jnp.where(pick, side[0], 0.0))
        size = 2
        while size < tokens:
            pick = (row // (2 * size) == col // (2 * size)) & (row // size != col // size)
            step = []
            index = 0
            for work in todo:
                for side in work[5]:
                    step.append(MM(inverse[index], jnp.where(pick, side[0], 0.0)))
                    index += 1
            inverse = [now + MM(part, now) for now, part in zip(inverse, step)]
            size *= 2

        for pair, (at, left_r, val, ends, fade, sides) in enumerate(todo):
            reads = [MM(inverse[2 * pair + head], sides[head][4]) for head in range(2)]
            both = reads[0] + reads[1]
            outs = once(
                jnp.concatenate([sides[0][1], sides[1][1]], 1), jnp.concatenate(reads, 0)
            )
            straight = once(
                jnp.concatenate([sides[0][2], sides[1][2]], 1),
                jnp.concatenate([sides[0][3], sides[1][3]], 0),
            )
            local_s[:, at] = outs[:, :LANES] + straight
            probe_s[:, at] = outs[:, LANES:] + left_r
            carry = once(both[:, LANES:], ends[:tokens], ROWS_ROWS)
            spot = chunk * PAIRS + pair
            trans_s[spot] = jnp.where(same_head, carry, 0.0) + jnp.where(diagonal, fade, 0.0)
            made = once(jnp.concatenate([both[:, :LANES], val], 0), ends, ROWS_ROWS)
            made = jnp.where(same_head, made, 0.0)
            own_s[spot] = made[:ATTN_GROUP_DIM] + made[ATTN_GROUP_DIM:]

    def finish(chunk):
        first = iota((tokens, LANES), 1) < ATTN_GROUP_DIM
        same_head = (iota((LANES, LANES), 0) < ATTN_GROUP_DIM) == (
            iota((LANES, LANES), 1) < ATTN_GROUP_DIM
        )
        for pair in range(PAIRS):
            at = lanes_of(chunk, pair)
            prior = arrive_s[chunk, pair]
            prior = jnp.where(same_head, jnp.concatenate([prior, prior], 0), 0.0)
            wkv = local_s[:, at] + once(probe_s[:, at], prior, COLS_COLS)
            center = wkv - head_sum(wkv, first) * (1.0 / ATTN_GROUP_DIM)
            spread = head_sum(center * center, first) * (1.0 / ATTN_GROUP_DIM)
            lines = center * lax.rsqrt(spread + 1e-05) * scale_ref[:, at] + shift_ref[:, at]
            bonus = head_sum(
                rec_ref[:, at].astype(F32) * key_ref[:, at].astype(F32) * reward_ref[:, at], first
            ) * val_ref[:, at].astype(F32)
            mixed = (lines + bonus).astype(BF16)
            mixed_ref[:, at] = mixed
            enc = (mixed.astype(F32) - center_ref[:, at]).astype(BF16)
            placed = once(spread_ref[...], enc).astype(BF16)
            stage_s[chunk, :, :, pair * LANES : (pair + 1) * LANES] = placed.reshape(
                devices, pair_rows, LANES
            )
        others(lambda other: row_copy(chunk, other, me).start())
        got_s[chunk, me] = stage_s[chunk, me]

    def chain(chunk):
        @pl.when(me == 0)
        def _():
            arrive_s[chunk] = jnp.zeros(arrive_s.shape[1:], F32)

        @pl.when(me > 0)
        def _():
            onward(chunk).wait_recv()

        @pl.when(me < devices - 1)
        def _():
            for pair in range(PAIRS):
                spot = chunk * PAIRS + pair
                leave_s[chunk, pair] = (
                    thrice(arrive_s[chunk, pair], trans_s[spot]) + own_s[spot]
                )
            onward(chunk).start()

        finish(chunk)

    def step(index, _):
        @pl.when(index < chunks)
        def _():
            local(index)

        late = index - me

        @pl.when((late >= 0) & (late < chunks))
        def _():
            chain(late)

        return 0

    lax.fori_loop(0, chunks + devices - 1, step, 0)

    table_copy.wait()
    others(lambda other: mask_copy(other, me, other).wait_recv())

    def chunk_at(chunk):
        return pl.ds(pl.multiple_of(chunk * chunk_lanes, chunk_lanes), chunk_lanes)

    def strip_at(strip):
        return pl.ds(pl.multiple_of(strip * STRIP, STRIP), STRIP)

    def encoded(chunk, strip):
        return lax.dot_general(
            got_s[chunk].reshape(rows, chunk_lanes),
            table_s[strip_at(strip), chunk_at(chunk)],
            COLS_COLS,
            preferred_element_type=F32,
        )

    def encode(chunk, _):
        others(lambda other: row_copy(chunk, me, other).wait_recv())

        def one(strip, _):
            @pl.when(chunk == 0)
            def _():
                pre_s[strip] = encoded(chunk, strip)

            @pl.when(chunk > 0)
            def _():
                pre_s[strip] += encoded(chunk, strip)

            @pl.when(chunk == chunks - 1)
            def _():
                half_s[strip] = pre_s[strip].astype(BF16)
                half_copy(strip).start()

            return 0

        lax.fori_loop(0, strips, one, 0)
        return 0

    lax.fori_loop(0, chunks, encode, 0)

    for strip in range(strips):
        half_copy(strip).wait_recv()
        for block in range(STRIP // BLK):
            inside = slice(block * BLK, (block + 1) * BLK)
            at = slice(strip * STRIP + block * BLK, strip * STRIP + (block + 1) * BLK)
            pre = pre_s[strip, :, inside] + peer_s[strip, :, inside].astype(F32)
            code = jnp.maximum(pre + bias_ref[:, at], 0.0)
            code = jnp.where(hit_ref[:, at] > 0.0, forced_ref[:, at], code)
            index = strip * (STRIP // BLK) + block
            active = mask_s[:, :, index : index + 1].reshape(rows, 1).astype(F32)
            codes_s[:, at] = (code * active).astype(BF16)

    def decode(chunk, _):
        part = lax.dot_general(
            codes_s[...], table_s[:, chunk_at(chunk)], ROWS_COLS, preferred_element_type=F32
        )
        part_s[chunk] = part.astype(BF16).reshape(devices, pair_rows, chunk_lanes)
        others(lambda other: part_copy(chunk, other, me).start())
        back_s[chunk, me] = part_s[chunk, me]
        return 0

    lax.fori_loop(0, chunks, decode, 0)

    def combine(chunk, _):
        others(lambda other: part_copy(chunk, me, other).wait_recv())
        at = chunk_at(chunk)
        total = lax.dot_general(
            gather_ref[...],
            back_s[chunk].reshape(rows, chunk_lanes),
            ROWS_COLS,
            preferred_element_type=F32,
        )
        steered_ref[:, at] = (total + center_ref[:, at]).astype(BF16)
        return 0

    lax.fori_loop(0, chunks, combine, 0)

    def drain(chunk, _):
        @pl.when(me < devices - 1)
        def _():
            onward(chunk).wait_send()

        others(lambda other: row_copy(chunk, other, me).wait_send())
        others(lambda other: part_copy(chunk, other, me).wait_send())
        return 0

    lax.fori_loop(0, chunks, drain, 0)
    others(lambda other: mask_copy(other, other, me).wait_send())
    for strip in range(strips):
        half_copy(strip).wait_send()


MM = thrice
STRIP = 512


def whole(devices, rec, key, val, rate, learn, lines, spread, gather, tile_mask, latent_lines, table):
    tokens, width = rec.shape
    chunks = width // (PAIRS * LANES)
    pairs = width // LANES
    latents = table.shape[0]
    rows = spread.shape[0]
    pair_rows = rows // devices
    strips = latents // STRIP
    shape = jax.ShapeDtypeStruct((tokens, width), BF16)
    vmem = pl.BlockSpec(memory_space=pltpu.VMEM)
    blocks = pltpu.VMEM((chunks, devices, pair_rows, PAIRS * LANES), BF16)
    strip_rows = pltpu.VMEM((strips, rows, STRIP), BF16)
    dma = pltpu.SemaphoreType.DMA
    return pl.pallas_call(
        functools.partial(whole_kernel, devices),
        out_shape=(shape, shape),
        in_specs=[vmem] * 15 + [pl.BlockSpec(memory_space=pl.ANY)],
        out_specs=(vmem, vmem),
        scratch_shapes=[
            pltpu.VMEM((tokens, width), F32),
            pltpu.VMEM((tokens, width), F32),
            pltpu.VMEM((pairs, LANES, LANES), F32),
            pltpu.VMEM((pairs, ATTN_GROUP_DIM, LANES), F32),
            pltpu.VMEM((chunks, PAIRS, ATTN_GROUP_DIM, LANES), F32),
            pltpu.VMEM((chunks, PAIRS, ATTN_GROUP_DIM, LANES), F32),
            pltpu.VMEM((latents, width), BF16),
            blocks,
            blocks,
            pltpu.VMEM((devices, pair_rows, LANES), BF16),
            pltpu.VMEM((strips, rows, STRIP), F32),
            strip_rows,
            strip_rows,
            pltpu.VMEM((rows, latents), BF16),
            blocks,
            blocks,
            dma((chunks,)),
            dma((chunks,)),
            dma,
            dma((chunks, devices)),
            dma((chunks, devices)),
            dma((devices,)),
            dma((devices,)),
            dma((strips,)),
            dma((strips,)),
            dma((chunks, devices)),
            dma((chunks, devices)),
        ],
        compiler_params=pltpu.CompilerParams(
            collective_id=0, has_side_effects=True, vmem_limit_bytes=52 * 1024 * 1024
        ),
        name="whole",
    )(rec, key, val, rate, learn, *lines, spread, gather, tile_mask, *latent_lines, table)


def body(
    gating_vectors,
    lookup_vectors,
    payload_vectors,
    forgetting_exponent,
    inline_adapt_factor,
    group_layer_scaling,
    group_layer_offset,
    present_reward_factor,
    shared_dictionary_matrix,
    sparse_code_offset,
    reconstruct_offset,
    panel_holder_choice,
    holder_group_enabled,
    fixed_feature_slot,
    fixed_feature_amount,
):
    tok_rows = gating_vectors.shape[0]
    ctx_count = lax.axis_size("ctx")
    tile_count = tok_rows // TILE
    slot_count = panel_holder_choice.shape[1]
    blocks_own = holder_group_enabled.shape[2]
    capacity = max(2, 2 * tok_rows * slot_count // (TILE * ctx_count))
    pair_count = tile_count * slot_count
    owner_flat = panel_holder_choice.reshape(pair_count)
    earlier = (owner_flat[:, None] == owner_flat[None, :]) & (
        iota((pair_count, pair_count), 1) < iota((pair_count, pair_count), 0)
    )
    ranks = jnp.sum(earlier.astype(jnp.int32), axis=1)
    slot_ids = owner_flat * capacity + ranks
    dispatch = (
        slot_ids[None, :] == lax.broadcasted_iota(jnp.int32, (ctx_count * capacity, 1), 0)
    ).astype(jnp.float32)
    tile_pick = (
        lax.broadcasted_iota(jnp.int32, (tile_count, pair_count), 1) // slot_count
        == lax.broadcasted_iota(jnp.int32, (tile_count, pair_count), 0)
    ).astype(jnp.float32)
    slot_tile = jnp.dot(dispatch, tile_pick.T)
    each = jnp.eye(TILE, dtype=jnp.float32)
    rows = ctx_count * capacity * TILE
    spread = (
        (slot_tile[:, None, :, None] * each[None, :, None, :])
        .reshape(rows, tok_rows)
        .astype(jnp.bfloat16)
    )
    tile_mask = jnp.dot(
        dispatch, holder_group_enabled.reshape(pair_count, blocks_own).astype(jnp.float32)
    )
    tile_mask = jnp.pad(tile_mask, ((0, 0), (0, LANES - blocks_own)))
    tile_mask = jnp.broadcast_to(tile_mask[:, None, :], (ctx_count * capacity, TILE, LANES))
    tile_mask = tile_mask.astype(jnp.bfloat16).reshape(ctx_count, capacity * TILE, LANES)
    within = lax.broadcasted_iota(jnp.int32, (blocks_own, BLK), 1)
    hit = (within == fixed_feature_slot[:, None]).astype(jnp.float32).reshape(1, -1)
    forced = jnp.broadcast_to(fixed_feature_amount[:, None], (blocks_own, BLK)).reshape(1, -1)
    lines = (group_layer_scaling, group_layer_offset, present_reward_factor, reconstruct_offset)
    return whole(
        ctx_count,
        gating_vectors,
        lookup_vectors,
        payload_vectors,
        forgetting_exponent,
        inline_adapt_factor,
        tuple(line[None] for line in lines),
        spread,
        spread.T,
        tile_mask,
        (sparse_code_offset[None], hit, forced),
        shared_dictionary_matrix,
    )


def solution(mesh):
    placed = (
        P(("groups", "ctx"), "width"),
        P(("groups", "ctx"), "width"),
        P(("groups", "ctx"), "width"),
        P(("groups", "ctx"), "width"),
        P(("groups", "ctx"), "width"),
        P("width"),
        P("width"),
        P("width"),
        P("ctx", "width"),
        P("ctx"),
        P("width"),
        P(("groups", "ctx"), None),
        P(("groups", "ctx"), None, None),
        P("ctx"),
        P("ctx"),
    )
    return jax.shard_map(
        body,
        mesh=mesh,
        in_specs=placed,
        out_specs=(P(("groups", "ctx"), "width"), P(("groups", "ctx"), "width")),
        check_vma=False,
    )
```

```python
import functools

import jax
import jax.numpy as jnp
from jax import lax
from jax.experimental import pallas as pl
from jax.experimental.pallas import tpu as pltpu
from jax.sharding import PartitionSpec as P

ATTN_GROUP_DIM = 64
TILE = 8
BLK = 128
LANES = 128
PAIRS = 2

HIGHEST = lax.Precision.HIGHEST
BF16 = jnp.bfloat16
F32 = jnp.float32
ROWS_COLS = (((1,), (0,)), ((), ()))
COLS_COLS = (((1,), (1,)), ((), ()))
ROWS_ROWS = (((0,), (0,)), ((), ()))


def once(a, b, dims=ROWS_COLS):
    return lax.dot_general(a.astype(BF16), b.astype(BF16), dims, preferred_element_type=F32)


def split(a):
    high = a.astype(BF16)
    return high, (a - high.astype(F32)).astype(BF16)


def fine(a, b):
    a_high, a_low = split(a)
    b_high, b_low = split(b)
    left = jnp.concatenate([a_high, a_low], 1)
    if b.shape[1] == LANES:
        right = jnp.concatenate([b_high, b_low], 1)
        both = once(left, jnp.concatenate([right, right], 0))
        return both[:, :LANES] + both[:, LANES:]
    return once(left, jnp.concatenate([b_high, b_high], 0)) + once(a_high, b_low)


def iota(shape, dim):
    return lax.broadcasted_iota(jnp.int32, shape, dim)


def head_sum(array, first):
    low = jnp.sum(jnp.where(first, array, 0.0), -1, keepdims=True)
    high = jnp.sum(jnp.where(first, 0.0, array), -1, keepdims=True)
    return jnp.where(first, low, high)


def whole_kernel(
    devices,
    rec_ref,
    key_ref,
    val_ref,
    rate_ref,
    learn_ref,
    scale_ref,
    shift_ref,
    reward_ref,
    center_ref,
    placing_ref,
    tile_mask_ref,
    bias_ref,
    hit_ref,
    forced_ref,
    table_ref,
    mixed_ref,
    steered_ref,
    local_s,
    probe_s,
    trans_s,
    own_s,
    arrive_s,
    leave_s,
    spread_s,
    gather_s,
    table_s,
    stage_s,
    got_s,
    mask_s,
    pre_s,
    half_s,
    peer_s,
    codes_s,
    part_s,
    back_s,
    send_sem,
    recv_sem,
    table_sem,
    out_sem,
    in_sem,
    mask_out_sem,
    mask_in_sem,
    half_out_sem,
    half_in_sem,
    part_out_sem,
    part_in_sem,
):
    me = lax.axis_index("ctx")
    peer = 1 - lax.axis_index("width")
    tokens, width = rec_ref.shape
    chunk_lanes = PAIRS * LANES
    chunks = width // chunk_lanes
    latents = bias_ref.shape[0] * BLK
    rows = placing_ref.shape[1]
    pair_rows = rows // devices
    strips = latents // STRIP

    table_copy = pltpu.make_async_copy(table_ref, table_s, table_sem)
    table_copy.start()

    barrier = pltpu.get_barrier_semaphore()

    def greet(hop, _):
        pl.semaphore_signal(
            barrier,
            inc=1,
            device_id={"ctx": lax.rem(me + hop, devices)},
            device_id_type=pl.DeviceIdType.MESH,
        )
        return 0

    lax.fori_loop(1, devices, greet, 0)
    pl.semaphore_signal(
        barrier, inc=1, device_id={"width": peer}, device_id_type=pl.DeviceIdType.MESH
    )
    pl.semaphore_wait(barrier, devices)

    def mask_copy(source, owner, sender):
        return pltpu.make_async_remote_copy(
            src_ref=tile_mask_ref.at[source],
            dst_ref=mask_s.at[sender],
            send_sem=mask_out_sem.at[owner],
            recv_sem=mask_in_sem.at[sender],
            device_id={"ctx": owner},
            device_id_type=pl.DeviceIdType.MESH,
        )

    def row_copy(chunk, owner, sender):
        return pltpu.make_async_remote_copy(
            src_ref=stage_s.at[chunk, owner],
            dst_ref=got_s.at[chunk, sender],
            send_sem=out_sem.at[chunk, owner],
            recv_sem=in_sem.at[chunk, sender],
            device_id={"ctx": owner},
            device_id_type=pl.DeviceIdType.MESH,
        )

    def part_copy(chunk, home, owner):
        return pltpu.make_async_remote_copy(
            src_ref=part_s.at[chunk, home],
            dst_ref=back_s.at[chunk, owner],
            send_sem=part_out_sem.at[chunk, home],
            recv_sem=part_in_sem.at[chunk, owner],
            device_id={"ctx": home},
            device_id_type=pl.DeviceIdType.MESH,
        )

    def half_copy(strip):
        return pltpu.make_async_remote_copy(
            src_ref=half_s.at[strip],
            dst_ref=peer_s.at[strip],
            send_sem=half_out_sem.at[strip],
            recv_sem=half_in_sem.at[strip],
            device_id={"width": peer},
            device_id_type=pl.DeviceIdType.MESH,
        )

    def others(visit):
        def hop_to(hop, _):
            visit(lax.rem(me + hop, devices))
            return 0

        lax.fori_loop(1, devices, hop_to, 0)

    others(lambda other: mask_copy(other, other, me).start())
    mask_s[me] = tile_mask_ref[me]
    gather = (placing_ref[...] == iota((tokens, rows), 0)).astype(F32)
    gather_s[...] = gather.astype(BF16)
    spread_s[...] = gather.T.astype(BF16)

    def lanes_of(chunk, pair):
        return pl.ds(pl.multiple_of(chunk * chunk_lanes + pair * LANES, LANES), LANES)

    def onward(chunk):
        return pltpu.make_async_remote_copy(
            src_ref=leave_s.at[chunk],
            dst_ref=arrive_s.at[chunk],
            send_sem=send_sem.at[chunk],
            recv_sem=recv_sem.at[chunk],
            device_id={"ctx": me + 1},
            device_id_type=pl.DeviceIdType.MESH,
        )

    def local(chunk):
        first = iota((tokens, LANES), 1) < ATTN_GROUP_DIM
        row = iota((tokens, tokens), 0)
        col = iota((tokens, tokens), 1)
        strict = row > col
        inclusive = row >= col
        same_head = (iota((LANES, LANES), 0) < ATTN_GROUP_DIM) == (
            iota((LANES, LANES), 1) < ATTN_GROUP_DIM
        )
        diagonal = iota((LANES, LANES), 0) == iota((LANES, LANES), 1)
        lower = inclusive.astype(F32).astype(BF16)
        identity = (row == col).astype(F32)

        todo = []
        for pair in range(PAIRS):
            at = lanes_of(chunk, pair)
            rec = rec_ref[:, at].astype(F32)
            key = key_ref[:, at].astype(F32)
            val = val_ref[:, at].astype(F32)
            rate = rate_ref[:, at].astype(F32)
            learn = learn_ref[:, at].astype(F32)
            total = lax.dot_general(
                lower, rate_ref[:, at], ROWS_COLS, preferred_element_type=F32
            )
            removal = key * lax.rsqrt(head_sum(key * key, first) + ATTN_GROUP_DIM * 1e-05)
            undo = jnp.exp(total)
            fade_to_end = jnp.exp(total - total[tokens - 1 :, :])
            left_a = -removal * jnp.exp(rate - total)
            left_r = rec * jnp.exp(-total)
            erase = removal * learn
            right = jnp.concatenate([erase * undo, key * undo], 0)
            ends = jnp.concatenate([erase * fade_to_end, key * fade_to_end], 0)
            fade = jnp.exp(-total[tokens - 1 :, :])
            right_high, right_low = split(right)
            right_twice = jnp.concatenate([right_high, right_high], 1)
            sides = []
            for head in range(2):
                mine = first if head == 0 else jnp.logical_not(first)
                left = jnp.concatenate(
                    [jnp.where(mine, left_a, 0.0), jnp.where(mine, left_r, 0.0)], 0
                )
                left_high, left_low = split(left)
                gram = once(
                    jnp.concatenate([left_high, left_low], 1), right_twice, COLS_COLS
                ) + once(left_high, right_low, COLS_COLS)
                mix_ab = jnp.where(strict, gram[:tokens, :tokens], 0.0)
                mix_ak = jnp.where(strict, gram[:tokens, tokens:], 0.0)
                mix_rb = jnp.where(inclusive, gram[tokens:, :tokens], 0.0)
                mix_rk = jnp.where(inclusive, gram[tokens:, tokens:], 0.0)
                own_val = jnp.where(mine, val, 0.0)
                target = jnp.concatenate(
                    [once(mix_ak, own_val), jnp.where(mine, left_a, 0.0)], 1
                )
                sides.append((mix_ab, mix_rb, mix_rk, own_val, target))
            todo.append((at, left_r, val, ends, fade, sides))

        inverse = []
        for work in todo:
            for side in work[5]:
                pick = (row // 2 == col // 2)
                inverse.append(identity + jnp.where(pick, side[0], 0.0))
        size = 2
        while size < tokens:
            pick = (row // (2 * size) == col // (2 * size)) & (row // size != col // size)
            step = []
            index = 0
            for work in todo:
                for side in work[5]:
                    step.append(fine(inverse[index], jnp.where(pick, side[0], 0.0)))
                    index += 1
            inverse = [now + fine(part, now) for now, part in zip(inverse, step)]
            size *= 2

        for pair, (at, left_r, val, ends, fade, sides) in enumerate(todo):
            reads = [fine(inverse[2 * pair + head], sides[head][4]) for head in range(2)]
            both = reads[0] + reads[1]
            outs = once(
                jnp.concatenate([sides[0][1], sides[1][1]], 1), jnp.concatenate(reads, 0)
            )
            straight = once(
                jnp.concatenate([sides[0][2], sides[1][2]], 1),
                jnp.concatenate([sides[0][3], sides[1][3]], 0),
            )
            local_s[:, at] = outs[:, :LANES] + straight
            probe_s[:, at] = outs[:, LANES:] + left_r
            carry = once(both[:, LANES:], ends[:tokens], ROWS_ROWS)
            spot = chunk * PAIRS + pair
            trans_s[spot] = jnp.where(same_head, carry, 0.0) + jnp.where(diagonal, fade, 0.0)
            made = once(jnp.concatenate([both[:, :LANES], val], 0), ends, ROWS_ROWS)
            made = jnp.where(same_head, made, 0.0)
            own_s[spot] = made[:ATTN_GROUP_DIM] + made[ATTN_GROUP_DIM:]

    def finish(chunk):
        first = iota((tokens, LANES), 1) < ATTN_GROUP_DIM
        same_head = (iota((LANES, LANES), 0) < ATTN_GROUP_DIM) == (
            iota((LANES, LANES), 1) < ATTN_GROUP_DIM
        )
        for pair in range(PAIRS):
            at = lanes_of(chunk, pair)
            prior = arrive_s[chunk, pair]
            prior = jnp.where(same_head, jnp.concatenate([prior, prior], 0), 0.0)
            wkv = local_s[:, at] + once(probe_s[:, at], prior, COLS_COLS)
            center = wkv - head_sum(wkv, first) * (1.0 / ATTN_GROUP_DIM)
            spread = head_sum(center * center, first) * (1.0 / ATTN_GROUP_DIM)
            lines = center * lax.rsqrt(spread + 1e-05) * scale_ref[:, at] + shift_ref[:, at]
            bonus = head_sum(
                rec_ref[:, at].astype(F32) * key_ref[:, at].astype(F32) * reward_ref[:, at], first
            ) * val_ref[:, at].astype(F32)
            mixed = (lines + bonus).astype(BF16)
            mixed_ref[:, at] = mixed
            enc = (mixed.astype(F32) - center_ref[:, at]).astype(BF16)
            placed = once(spread_s[...], enc).astype(BF16)
            stage_s[chunk, :, :, pair * LANES : (pair + 1) * LANES] = placed.reshape(
                devices, pair_rows, LANES
            )
        others(lambda other: row_copy(chunk, other, me).start())
        got_s[chunk, me] = stage_s[chunk, me]

    def chain(chunk):
        @pl.when(me == 0)
        def _():
            arrive_s[chunk] = jnp.zeros(arrive_s.shape[1:], F32)

        @pl.when(me > 0)
        def _():
            onward(chunk).wait_recv()

        @pl.when(me < devices - 1)
        def _():
            for pair in range(PAIRS):
                spot = chunk * PAIRS + pair
                leave_s[chunk, pair] = (
                    fine(arrive_s[chunk, pair], trans_s[spot]) + own_s[spot]
                )
            onward(chunk).start()

        finish(chunk)

    def step(index, _):
        @pl.when(index < chunks)
        def _():
            local(index)

        late = index - me

        @pl.when((late >= 0) & (late < chunks))
        def _():
            chain(late)

        return 0

    lax.fori_loop(0, chunks + devices - 1, step, 0)

    table_copy.wait()
    others(lambda other: mask_copy(other, me, other).wait_recv())

    def chunk_at(chunk):
        return pl.ds(pl.multiple_of(chunk * chunk_lanes, chunk_lanes), chunk_lanes)

    def strip_at(strip):
        return pl.ds(pl.multiple_of(strip * STRIP, STRIP), STRIP)

    def encoded(chunk, strip):
        return lax.dot_general(
            got_s[chunk].reshape(rows, chunk_lanes),
            table_s[strip_at(strip), chunk_at(chunk)],
            COLS_COLS,
            preferred_element_type=F32,
        )

    def encode(chunk, _):
        others(lambda other: row_copy(chunk, me, other).wait_recv())

        def one(strip, _):
            @pl.when(chunk == 0)
            def _():
                pre_s[strip] = encoded(chunk, strip)

            @pl.when(chunk > 0)
            def _():
                pre_s[strip] += encoded(chunk, strip)

            @pl.when(chunk == chunks - 1)
            def _():
                half_s[strip] = pre_s[strip].astype(BF16)
                half_copy(strip).start()

            return 0

        lax.fori_loop(0, strips, one, 0)
        return 0

    lax.fori_loop(0, chunks, encode, 0)

    for strip in range(strips):
        half_copy(strip).wait_recv()
        for block in range(STRIP // BLK):
            inside = slice(block * BLK, (block + 1) * BLK)
            at = slice(strip * STRIP + block * BLK, strip * STRIP + (block + 1) * BLK)
            index = strip * (STRIP // BLK) + block
            line = slice(index, index + 1)
            pre = pre_s[strip, :, inside] + peer_s[strip, :, inside].astype(F32)
            code = jnp.maximum(pre + bias_ref[line, :], 0.0)
            code = jnp.where(hit_ref[line, :] > 0.0, forced_ref[line, :], code)
            active = mask_s[:, :, index : index + 1].reshape(rows, 1).astype(F32)
            codes_s[:, at] = (code * active).astype(BF16)

    def decode(chunk, _):
        part = lax.dot_general(
            codes_s[...], table_s[:, chunk_at(chunk)], ROWS_COLS, preferred_element_type=F32
        )
        part_s[chunk] = part.astype(BF16).reshape(devices, pair_rows, chunk_lanes)
        others(lambda other: part_copy(chunk, other, me).start())
        back_s[chunk, me] = part_s[chunk, me]
        return 0

    lax.fori_loop(0, chunks, decode, 0)

    def combine(chunk, _):
        others(lambda other: part_copy(chunk, me, other).wait_recv())
        at = chunk_at(chunk)
        total = lax.dot_general(
            gather_s[...],
            back_s[chunk].reshape(rows, chunk_lanes),
            ROWS_COLS,
            preferred_element_type=F32,
        )
        steered_ref[:, at] = (total + center_ref[:, at]).astype(BF16)
        return 0

    lax.fori_loop(0, chunks, combine, 0)

    def drain(chunk, _):
        @pl.when(me < devices - 1)
        def _():
            onward(chunk).wait_send()

        others(lambda other: row_copy(chunk, other, me).wait_send())
        others(lambda other: part_copy(chunk, other, me).wait_send())
        return 0

    lax.fori_loop(0, chunks, drain, 0)
    others(lambda other: mask_copy(other, other, me).wait_send())
    for strip in range(strips):
        half_copy(strip).wait_send()


STRIP = 512


def whole(devices, rec, key, val, rate, learn, lines, placing, tile_mask, latent_lines, table):
    tokens, width = rec.shape
    chunks = width // (PAIRS * LANES)
    pairs = width // LANES
    latents = table.shape[0]
    rows = placing.shape[1]
    pair_rows = rows // devices
    strips = latents // STRIP
    shape = jax.ShapeDtypeStruct((tokens, width), BF16)
    vmem = pl.BlockSpec(memory_space=pltpu.VMEM)
    blocks = pltpu.VMEM((chunks, devices, pair_rows, PAIRS * LANES), BF16)
    strip_rows = pltpu.VMEM((strips, rows, STRIP), BF16)
    dma = pltpu.SemaphoreType.DMA
    return pl.pallas_call(
        functools.partial(whole_kernel, devices),
        out_shape=(shape, shape),
        in_specs=[vmem] * 14 + [pl.BlockSpec(memory_space=pl.ANY)],
        out_specs=(vmem, vmem),
        scratch_shapes=[
            pltpu.VMEM((tokens, width), F32),
            pltpu.VMEM((tokens, width), F32),
            pltpu.VMEM((pairs, LANES, LANES), F32),
            pltpu.VMEM((pairs, ATTN_GROUP_DIM, LANES), F32),
            pltpu.VMEM((chunks, PAIRS, ATTN_GROUP_DIM, LANES), F32),
            pltpu.VMEM((chunks, PAIRS, ATTN_GROUP_DIM, LANES), F32),
            pltpu.VMEM((rows, tokens), BF16),
            pltpu.VMEM((tokens, rows), BF16),
            pltpu.VMEM((latents, width), BF16),
            blocks,
            blocks,
            pltpu.VMEM((devices, pair_rows, LANES), BF16),
            pltpu.VMEM((strips, rows, STRIP), F32),
            strip_rows,
            strip_rows,
            pltpu.VMEM((rows, latents), BF16),
            blocks,
            blocks,
            dma((chunks,)),
            dma((chunks,)),
            dma,
            dma((chunks, devices)),
            dma((chunks, devices)),
            dma((devices,)),
            dma((devices,)),
            dma((strips,)),
            dma((strips,)),
            dma((chunks, devices)),
            dma((chunks, devices)),
        ],
        compiler_params=pltpu.CompilerParams(
            collective_id=0, has_side_effects=True, vmem_limit_bytes=52 * 1024 * 1024
        ),
        name="whole",
    )(rec, key, val, rate, learn, *lines, placing, tile_mask, *latent_lines, table)


def body(
    gating_vectors,
    lookup_vectors,
    payload_vectors,
    forgetting_exponent,
    inline_adapt_factor,
    group_layer_scaling,
    group_layer_offset,
    present_reward_factor,
    shared_dictionary_matrix,
    sparse_code_offset,
    reconstruct_offset,
    panel_holder_choice,
    holder_group_enabled,
    fixed_feature_slot,
    fixed_feature_amount,
):
    tok_rows = gating_vectors.shape[0]
    ctx_count = lax.axis_size("ctx")
    tile_count = tok_rows // TILE
    slot_count = panel_holder_choice.shape[1]
    blocks_own = holder_group_enabled.shape[2]
    capacity = max(2, 2 * tok_rows * slot_count // (TILE * ctx_count))
    pair_count = tile_count * slot_count
    owner_flat = panel_holder_choice.reshape(pair_count)
    earlier = (owner_flat[:, None] == owner_flat[None, :]) & (
        iota((pair_count, pair_count), 1) < iota((pair_count, pair_count), 0)
    )
    ranks = jnp.sum(earlier.astype(jnp.int32), axis=1)
    slot_ids = owner_flat * capacity + ranks
    named = slot_ids[None, :] == lax.broadcasted_iota(jnp.int32, (ctx_count * capacity, 1), 0)
    dispatch = named.astype(jnp.float32)
    rows = ctx_count * capacity * TILE
    tile_of_pair = lax.broadcasted_iota(jnp.int32, (1, pair_count), 1) // slot_count
    tile_of_slot = jnp.sum(jnp.where(named, tile_of_pair + 1, 0), axis=1) - 1
    step = lax.broadcasted_iota(jnp.int32, (1, TILE), 1)
    placing = jnp.where(tile_of_slot[:, None] < 0, -1, tile_of_slot[:, None] * TILE + step)
    placing = placing.reshape(1, rows)
    tile_mask = jnp.dot(
        dispatch, holder_group_enabled.reshape(pair_count, blocks_own).astype(jnp.float32)
    )
    tile_mask = jnp.pad(tile_mask, ((0, 0), (0, LANES - blocks_own)))
    tile_mask = jnp.broadcast_to(tile_mask[:, None, :], (ctx_count * capacity, TILE, LANES))
    tile_mask = tile_mask.astype(jnp.bfloat16).reshape(ctx_count, capacity * TILE, LANES)
    within = lax.broadcasted_iota(jnp.int32, (blocks_own, BLK), 1)
    hit = (within == fixed_feature_slot[:, None]).astype(jnp.float32)
    forced = jnp.broadcast_to(fixed_feature_amount[:, None], (blocks_own, BLK))
    lines = (group_layer_scaling, group_layer_offset, present_reward_factor, reconstruct_offset)
    return whole(
        ctx_count,
        gating_vectors,
        lookup_vectors,
        payload_vectors,
        forgetting_exponent,
        inline_adapt_factor,
        tuple(line[None] for line in lines),
        placing,
        tile_mask,
        (sparse_code_offset.reshape(blocks_own, BLK), hit, forced),
        shared_dictionary_matrix,
    )


def solution(mesh):
    placed = (
        P(("groups", "ctx"), "width"),
        P(("groups", "ctx"), "width"),
        P(("groups", "ctx"), "width"),
        P(("groups", "ctx"), "width"),
        P(("groups", "ctx"), "width"),
        P("width"),
        P("width"),
        P("width"),
        P("ctx", "width"),
        P("ctx"),
        P("width"),
        P(("groups", "ctx"), None),
        P(("groups", "ctx"), None, None),
        P("ctx"),
        P("ctx"),
    )
    return jax.shard_map(
        body,
        mesh=mesh,
        in_specs=placed,
        out_specs=(P(("groups", "ctx"), "width"), P(("groups", "ctx"), "width")),
        check_vma=False,
    )
```

```python
import functools

import jax
import jax.numpy as jnp
from jax import lax
from jax.experimental import pallas as pl
from jax.experimental.pallas import tpu as pltpu
from jax.sharding import PartitionSpec as P

ATTN_GROUP_DIM = 64
TILE = 8
BLK = 128
LANES = 128
PAIRS = 2

HIGHEST = lax.Precision.HIGHEST
BF16 = jnp.bfloat16
F32 = jnp.float32
ROWS_COLS = (((1,), (0,)), ((), ()))
COLS_COLS = (((1,), (1,)), ((), ()))
ROWS_ROWS = (((0,), (0,)), ((), ()))


def once(a, b, dims=ROWS_COLS):
    return lax.dot_general(a.astype(BF16), b.astype(BF16), dims, preferred_element_type=F32)


def split(a):
    high = a.astype(BF16)
    return high, (a - high.astype(F32)).astype(BF16)


def thrice(a, b, dims=ROWS_COLS):
    a_high, a_low = split(a)
    b_high, b_low = split(b)
    dot = functools.partial(lax.dot_general, dimension_numbers=dims, preferred_element_type=F32)
    return dot(a_high, b_high) + (dot(a_high, b_low) + dot(a_low, b_high))


def iota(shape, dim):
    return lax.broadcasted_iota(jnp.int32, shape, dim)


def head_sum(array, first):
    low = jnp.sum(jnp.where(first, array, 0.0), -1, keepdims=True)
    high = jnp.sum(jnp.where(first, 0.0, array), -1, keepdims=True)
    return jnp.where(first, low, high)


def whole_kernel(
    devices,
    rec_ref,
    key_ref,
    val_ref,
    rate_ref,
    learn_ref,
    scale_ref,
    shift_ref,
    reward_ref,
    center_ref,
    placing_ref,
    tile_mask_ref,
    bias_ref,
    hit_ref,
    forced_ref,
    table_ref,
    mixed_ref,
    steered_ref,
    local_s,
    probe_s,
    trans_s,
    own_s,
    arrive_s,
    leave_s,
    spread_s,
    gather_s,
    table_s,
    stage_s,
    got_s,
    mask_s,
    pre_s,
    half_s,
    peer_s,
    codes_s,
    part_s,
    back_s,
    send_sem,
    recv_sem,
    table_sem,
    out_sem,
    in_sem,
    mask_out_sem,
    mask_in_sem,
    half_out_sem,
    half_in_sem,
    part_out_sem,
    part_in_sem,
):
    me = lax.axis_index("ctx")
    peer = 1 - lax.axis_index("width")
    tokens, width = rec_ref.shape
    chunk_lanes = PAIRS * LANES
    chunks = width // chunk_lanes
    latents = bias_ref.shape[0] * BLK
    rows = placing_ref.shape[1]
    pair_rows = rows // devices
    strips = latents // STRIP

    table_copy = pltpu.make_async_copy(table_ref, table_s, table_sem)
    table_copy.start()

    barrier = pltpu.get_barrier_semaphore()

    def greet(hop, _):
        pl.semaphore_signal(
            barrier,
            inc=1,
            device_id={"ctx": lax.rem(me + hop, devices)},
            device_id_type=pl.DeviceIdType.MESH,
        )
        return 0

    lax.fori_loop(1, devices, greet, 0)
    pl.semaphore_signal(
        barrier, inc=1, device_id={"width": peer}, device_id_type=pl.DeviceIdType.MESH
    )
    pl.semaphore_wait(barrier, devices)

    def mask_copy(source, owner, sender):
        return pltpu.make_async_remote_copy(
            src_ref=tile_mask_ref.at[source],
            dst_ref=mask_s.at[sender],
            send_sem=mask_out_sem.at[owner],
            recv_sem=mask_in_sem.at[sender],
            device_id={"ctx": owner},
            device_id_type=pl.DeviceIdType.MESH,
        )

    def row_copy(chunk, owner, sender):
        return pltpu.make_async_remote_copy(
            src_ref=stage_s.at[chunk, owner],
            dst_ref=got_s.at[chunk, sender],
            send_sem=out_sem.at[chunk, owner],
            recv_sem=in_sem.at[chunk, sender],
            device_id={"ctx": owner},
            device_id_type=pl.DeviceIdType.MESH,
        )

    def part_copy(chunk, home, owner):
        return pltpu.make_async_remote_copy(
            src_ref=part_s.at[chunk, home],
            dst_ref=back_s.at[chunk, owner],
            send_sem=part_out_sem.at[chunk, home],
            recv_sem=part_in_sem.at[chunk, owner],
            device_id={"ctx": home},
            device_id_type=pl.DeviceIdType.MESH,
        )

    def half_copy(strip):
        return pltpu.make_async_remote_copy(
            src_ref=half_s.at[strip],
            dst_ref=peer_s.at[strip],
            send_sem=half_out_sem.at[strip],
            recv_sem=half_in_sem.at[strip],
            device_id={"width": peer},
            device_id_type=pl.DeviceIdType.MESH,
        )

    def others(visit):
        def hop_to(hop, _):
            visit(lax.rem(me + hop, devices))
            return 0

        lax.fori_loop(1, devices, hop_to, 0)

    others(lambda other: mask_copy(other, other, me).start())
    mask_s[me] = tile_mask_ref[me]
    gather = (placing_ref[...] == iota((tokens, rows), 0)).astype(F32)
    gather_s[...] = gather.astype(BF16)
    spread_s[...] = gather.T.astype(BF16)

    def lanes_of(chunk, pair):
        return pl.ds(pl.multiple_of(chunk * chunk_lanes + pair * LANES, LANES), LANES)

    def onward(chunk):
        return pltpu.make_async_remote_copy(
            src_ref=leave_s.at[chunk],
            dst_ref=arrive_s.at[chunk],
            send_sem=send_sem.at[chunk],
            recv_sem=recv_sem.at[chunk],
            device_id={"ctx": me + 1},
            device_id_type=pl.DeviceIdType.MESH,
        )

    def local(chunk):
        first = iota((tokens, LANES), 1) < ATTN_GROUP_DIM
        row = iota((tokens, tokens), 0)
        col = iota((tokens, tokens), 1)
        strict = row > col
        inclusive = row >= col
        same_head = (iota((LANES, LANES), 0) < ATTN_GROUP_DIM) == (
            iota((LANES, LANES), 1) < ATTN_GROUP_DIM
        )
        diagonal = iota((LANES, LANES), 0) == iota((LANES, LANES), 1)
        lower = inclusive.astype(F32).astype(BF16)
        identity = (row == col).astype(F32)

        todo = []
        for pair in range(PAIRS):
            at = lanes_of(chunk, pair)
            rec = rec_ref[:, at].astype(F32)
            key = key_ref[:, at].astype(F32)
            val = val_ref[:, at].astype(F32)
            rate = rate_ref[:, at].astype(F32)
            learn = learn_ref[:, at].astype(F32)
            total = lax.dot_general(
                lower, rate_ref[:, at], ROWS_COLS, preferred_element_type=F32
            )
            removal = key * lax.rsqrt(head_sum(key * key, first) + ATTN_GROUP_DIM * 1e-05)
            undo = jnp.exp(total)
            fade_to_end = jnp.exp(total - total[tokens - 1 :, :])
            left_a = -removal * jnp.exp(rate - total)
            left_r = rec * jnp.exp(-total)
            erase = removal * learn
            right = jnp.concatenate([erase * undo, key * undo], 0)
            ends = jnp.concatenate([erase * fade_to_end, key * fade_to_end], 0)
            fade = jnp.exp(-total[tokens - 1 :, :])
            sides = []
            for head in range(2):
                mine = first if head == 0 else jnp.logical_not(first)
                left = jnp.concatenate(
                    [jnp.where(mine, left_a, 0.0), jnp.where(mine, left_r, 0.0)], 0
                )
                gram = once(left, right, COLS_COLS)
                mix_ab = jnp.where(strict, gram[:tokens, :tokens], 0.0)
                mix_ak = jnp.where(strict, gram[:tokens, tokens:], 0.0)
                mix_rb = jnp.where(inclusive, gram[tokens:, :tokens], 0.0)
                mix_rk = jnp.where(inclusive, gram[tokens:, tokens:], 0.0)
                own_val = jnp.where(mine, val, 0.0)
                target = jnp.concatenate(
                    [once(mix_ak, own_val), jnp.where(mine, left_a, 0.0)], 1
                )
                sides.append((mix_ab, mix_rb, mix_rk, own_val, target))
            todo.append((at, left_r, val, ends, fade, sides))

        inverse = []
        for work in todo:
            for side in work[5]:
                pick = (row // 2 == col // 2)
                inverse.append(identity + jnp.where(pick, side[0], 0.0))
        size = 2
        while size < tokens:
            pick = (row // (2 * size) == col // (2 * size)) & (row // size != col // size)
            step = []
            index = 0
            for work in todo:
                for side in work[5]:
                    step.append(once(inverse[index], jnp.where(pick, side[0], 0.0)))
                    index += 1
            inverse = [now + once(part, now) for now, part in zip(inverse, step)]
            size *= 2

        for pair, (at, left_r, val, ends, fade, sides) in enumerate(todo):
            reads = [once(inverse[2 * pair + head], sides[head][4]) for head in range(2)]
            both = reads[0] + reads[1]
            outs = once(
                jnp.concatenate([sides[0][1], sides[1][1]], 1), jnp.concatenate(reads, 0)
            )
            straight = once(
                jnp.concatenate([sides[0][2], sides[1][2]], 1),
                jnp.concatenate([sides[0][3], sides[1][3]], 0),
            )
            local_s[:, at] = outs[:, :LANES] + straight
            probe_s[:, at] = outs[:, LANES:] + left_r
            carry = once(both[:, LANES:], ends[:tokens], ROWS_ROWS)
            spot = chunk * PAIRS + pair
            trans_s[spot] = jnp.where(same_head, carry, 0.0) + jnp.where(diagonal, fade, 0.0)
            made = once(jnp.concatenate([both[:, :LANES], val], 0), ends, ROWS_ROWS)
            made = jnp.where(same_head, made, 0.0)
            own_s[spot] = made[:ATTN_GROUP_DIM] + made[ATTN_GROUP_DIM:]

    def finish(chunk):
        first = iota((tokens, LANES), 1) < ATTN_GROUP_DIM
        same_head = (iota((LANES, LANES), 0) < ATTN_GROUP_DIM) == (
            iota((LANES, LANES), 1) < ATTN_GROUP_DIM
        )
        for pair in range(PAIRS):
            at = lanes_of(chunk, pair)
            prior = arrive_s[chunk, pair].astype(F32)
            prior = jnp.where(same_head, jnp.concatenate([prior, prior], 0), 0.0)
            wkv = local_s[:, at] + once(probe_s[:, at], prior, COLS_COLS)
            center = wkv - head_sum(wkv, first) * (1.0 / ATTN_GROUP_DIM)
            spread = head_sum(center * center, first) * (1.0 / ATTN_GROUP_DIM)
            lines = center * lax.rsqrt(spread + 1e-05) * scale_ref[:, at] + shift_ref[:, at]
            bonus = head_sum(
                rec_ref[:, at].astype(F32) * key_ref[:, at].astype(F32) * reward_ref[:, at], first
            ) * val_ref[:, at].astype(F32)
            mixed = (lines + bonus).astype(BF16)
            mixed_ref[:, at] = mixed
            enc = (mixed.astype(F32) - center_ref[:, at]).astype(BF16)
            placed = once(spread_s[...], enc).astype(BF16)
            stage_s[chunk, :, :, pair * LANES : (pair + 1) * LANES] = placed.reshape(
                devices, pair_rows, LANES
            )
        others(lambda other: row_copy(chunk, other, me).start())
        got_s[chunk, me] = stage_s[chunk, me]

    def chain(chunk):
        @pl.when(me == 0)
        def _():
            arrive_s[chunk] = jnp.zeros(arrive_s.shape[1:], BF16)

        @pl.when(me > 0)
        def _():
            onward(chunk).wait_recv()

        @pl.when(me < devices - 1)
        def _():
            for pair in range(PAIRS):
                spot = chunk * PAIRS + pair
                leave_s[chunk, pair] = (
                    thrice(arrive_s[chunk, pair].astype(F32), trans_s[spot]) + own_s[spot]
                ).astype(BF16)
            onward(chunk).start()

        finish(chunk)

    def step(index, _):
        @pl.when(index < chunks)
        def _():
            local(index)

        late = index - me

        @pl.when((late >= 0) & (late < chunks))
        def _():
            chain(late)

        return 0

    lax.fori_loop(0, chunks + devices - 1, step, 0)

    table_copy.wait()
    others(lambda other: mask_copy(other, me, other).wait_recv())

    def chunk_at(chunk):
        return pl.ds(pl.multiple_of(chunk * chunk_lanes, chunk_lanes), chunk_lanes)

    def strip_at(strip):
        return pl.ds(pl.multiple_of(strip * STRIP, STRIP), STRIP)

    def encoded(chunk, strip):
        return lax.dot_general(
            got_s[chunk].reshape(rows, chunk_lanes),
            table_s[strip_at(strip), chunk_at(chunk)],
            COLS_COLS,
            preferred_element_type=F32,
        )

    def encode(chunk, _):
        others(lambda other: row_copy(chunk, me, other).wait_recv())

        def one(strip, _):
            @pl.when(chunk == 0)
            def _():
                pre_s[strip] = encoded(chunk, strip)

            @pl.when(chunk > 0)
            def _():
                pre_s[strip] += encoded(chunk, strip)

            @pl.when(chunk == chunks - 1)
            def _():
                half_s[strip] = pre_s[strip].astype(BF16)
                half_copy(strip).start()

            return 0

        lax.fori_loop(0, strips, one, 0)
        return 0

    lax.fori_loop(0, chunks, encode, 0)

    for strip in range(strips):
        half_copy(strip).wait_recv()
        for block in range(STRIP // BLK):
            inside = slice(block * BLK, (block + 1) * BLK)
            at = slice(strip * STRIP + block * BLK, strip * STRIP + (block + 1) * BLK)
            index = strip * (STRIP // BLK) + block
            line = slice(index, index + 1)
            pre = pre_s[strip, :, inside] + peer_s[strip, :, inside].astype(F32)
            code = jnp.maximum(pre + bias_ref[line, :], 0.0)
            code = jnp.where(hit_ref[line, :] > 0.0, forced_ref[line, :], code)
            active = mask_s[:, :, index : index + 1].reshape(rows, 1).astype(F32)
            codes_s[:, at] = (code * active).astype(BF16)

    def decode(chunk, _):
        part = lax.dot_general(
            codes_s[...], table_s[:, chunk_at(chunk)], ROWS_COLS, preferred_element_type=F32
        )
        part_s[chunk] = part.astype(BF16).reshape(devices, pair_rows, chunk_lanes)
        others(lambda other: part_copy(chunk, other, me).start())
        back_s[chunk, me] = part_s[chunk, me]
        return 0

    lax.fori_loop(0, chunks, decode, 0)

    def combine(chunk, _):
        others(lambda other: part_copy(chunk, me, other).wait_recv())
        at = chunk_at(chunk)
        total = lax.dot_general(
            gather_s[...],
            back_s[chunk].reshape(rows, chunk_lanes),
            ROWS_COLS,
            preferred_element_type=F32,
        )
        steered_ref[:, at] = (total + center_ref[:, at]).astype(BF16)
        return 0

    lax.fori_loop(0, chunks, combine, 0)

    def drain(chunk, _):
        @pl.when(me < devices - 1)
        def _():
            onward(chunk).wait_send()

        others(lambda other: row_copy(chunk, other, me).wait_send())
        others(lambda other: part_copy(chunk, other, me).wait_send())
        return 0

    lax.fori_loop(0, chunks, drain, 0)
    others(lambda other: mask_copy(other, other, me).wait_send())
    for strip in range(strips):
        half_copy(strip).wait_send()


STRIP = 512


def whole(devices, rec, key, val, rate, learn, lines, placing, tile_mask, latent_lines, table):
    tokens, width = rec.shape
    chunks = width // (PAIRS * LANES)
    pairs = width // LANES
    latents = table.shape[0]
    rows = placing.shape[1]
    pair_rows = rows // devices
    strips = latents // STRIP
    shape = jax.ShapeDtypeStruct((tokens, width), BF16)
    vmem = pl.BlockSpec(memory_space=pltpu.VMEM)
    blocks = pltpu.VMEM((chunks, devices, pair_rows, PAIRS * LANES), BF16)
    strip_rows = pltpu.VMEM((strips, rows, STRIP), BF16)
    dma = pltpu.SemaphoreType.DMA
    return pl.pallas_call(
        functools.partial(whole_kernel, devices),
        out_shape=(shape, shape),
        in_specs=[vmem] * 14 + [pl.BlockSpec(memory_space=pl.ANY)],
        out_specs=(vmem, vmem),
        scratch_shapes=[
            pltpu.VMEM((tokens, width), F32),
            pltpu.VMEM((tokens, width), F32),
            pltpu.VMEM((pairs, LANES, LANES), F32),
            pltpu.VMEM((pairs, ATTN_GROUP_DIM, LANES), F32),
            pltpu.VMEM((chunks, PAIRS, ATTN_GROUP_DIM, LANES), BF16),
            pltpu.VMEM((chunks, PAIRS, ATTN_GROUP_DIM, LANES), BF16),
            pltpu.VMEM((rows, tokens), BF16),
            pltpu.VMEM((tokens, rows), BF16),
            pltpu.VMEM((latents, width), BF16),
            blocks,
            blocks,
            pltpu.VMEM((devices, pair_rows, LANES), BF16),
            pltpu.VMEM((strips, rows, STRIP), F32),
            strip_rows,
            strip_rows,
            pltpu.VMEM((rows, latents), BF16),
            blocks,
            blocks,
            dma((chunks,)),
            dma((chunks,)),
            dma,
            dma((chunks, devices)),
            dma((chunks, devices)),
            dma((devices,)),
            dma((devices,)),
            dma((strips,)),
            dma((strips,)),
            dma((chunks, devices)),
            dma((chunks, devices)),
        ],
        compiler_params=pltpu.CompilerParams(
            collective_id=0, has_side_effects=True, vmem_limit_bytes=52 * 1024 * 1024
        ),
        name="whole",
    )(rec, key, val, rate, learn, *lines, placing, tile_mask, *latent_lines, table)


def body(
    gating_vectors,
    lookup_vectors,
    payload_vectors,
    forgetting_exponent,
    inline_adapt_factor,
    group_layer_scaling,
    group_layer_offset,
    present_reward_factor,
    shared_dictionary_matrix,
    sparse_code_offset,
    reconstruct_offset,
    panel_holder_choice,
    holder_group_enabled,
    fixed_feature_slot,
    fixed_feature_amount,
):
    tok_rows = gating_vectors.shape[0]
    ctx_count = lax.axis_size("ctx")
    tile_count = tok_rows // TILE
    slot_count = panel_holder_choice.shape[1]
    blocks_own = holder_group_enabled.shape[2]
    capacity = max(2, 2 * tok_rows * slot_count // (TILE * ctx_count))
    pair_count = tile_count * slot_count
    owner_flat = panel_holder_choice.reshape(pair_count)
    earlier = (owner_flat[:, None] == owner_flat[None, :]) & (
        iota((pair_count, pair_count), 1) < iota((pair_count, pair_count), 0)
    )
    ranks = jnp.sum(earlier.astype(jnp.int32), axis=1)
    slot_ids = owner_flat * capacity + ranks
    named = slot_ids[None, :] == lax.broadcasted_iota(jnp.int32, (ctx_count * capacity, 1), 0)
    dispatch = named.astype(jnp.float32)
    rows = ctx_count * capacity * TILE
    tile_of_pair = lax.broadcasted_iota(jnp.int32, (1, pair_count), 1) // slot_count
    tile_of_slot = jnp.sum(jnp.where(named, tile_of_pair + 1, 0), axis=1) - 1
    step = lax.broadcasted_iota(jnp.int32, (1, TILE), 1)
    placing = jnp.where(tile_of_slot[:, None] < 0, -1, tile_of_slot[:, None] * TILE + step)
    placing = placing.reshape(1, rows)
    tile_mask = jnp.dot(
        dispatch, holder_group_enabled.reshape(pair_count, blocks_own).astype(jnp.float32)
    )
    tile_mask = jnp.pad(tile_mask, ((0, 0), (0, LANES - blocks_own)))
    tile_mask = jnp.broadcast_to(tile_mask[:, None, :], (ctx_count * capacity, TILE, LANES))
    tile_mask = tile_mask.astype(jnp.bfloat16).reshape(ctx_count, capacity * TILE, LANES)
    within = lax.broadcasted_iota(jnp.int32, (blocks_own, BLK), 1)
    hit = (within == fixed_feature_slot[:, None]).astype(jnp.float32)
    forced = jnp.broadcast_to(fixed_feature_amount[:, None], (blocks_own, BLK))
    lines = (group_layer_scaling, group_layer_offset, present_reward_factor, reconstruct_offset)
    return whole(
        ctx_count,
        gating_vectors,
        lookup_vectors,
        payload_vectors,
        forgetting_exponent,
        inline_adapt_factor,
        tuple(line[None] for line in lines),
        placing,
        tile_mask,
        (sparse_code_offset.reshape(blocks_own, BLK), hit, forced),
        shared_dictionary_matrix,
    )


def solution(mesh):
    placed = (
        P(("groups", "ctx"), "width"),
        P(("groups", "ctx"), "width"),
        P(("groups", "ctx"), "width"),
        P(("groups", "ctx"), "width"),
        P(("groups", "ctx"), "width"),
        P("width"),
        P("width"),
        P("width"),
        P("ctx", "width"),
        P("ctx"),
        P("width"),
        P(("groups", "ctx"), None),
        P(("groups", "ctx"), None, None),
        P("ctx"),
        P("ctx"),
    )
    return jax.shard_map(
        body,
        mesh=mesh,
        in_specs=placed,
        out_specs=(P(("groups", "ctx"), "width"), P(("groups", "ctx"), "width")),
        check_vma=False,
    )
```
